256 devices in a mesh: clip: 2 (over core), ctx: 16 (over y, x), head: 8 (over z).
Axes of the slice: x: 4, y: 4, z: 8, core: 2. Of those that a mesh axis runs over, the one named last changes fastest.
Arguments:
- queries: bfloat16 [16384, 24, 128], P(('clip', 'ctx', 'head')), parts along dimension 0
- key_rows: bfloat16 [16384, 24, 128], P(('clip', 'ctx', 'head')), parts along dimension 0
- values: bfloat16 [16384, 24, 128], P(('clip', 'ctx', 'head')), parts along dimension 0, may hold values from -6 to 6
- query_tan: bfloat16 [16384, 24, 128], P(('clip', 'ctx', 'head')), parts along dimension 0, may hold values from -6 to 6
- key_tan: bfloat16 [16384, 24, 128], P(('clip', 'ctx', 'head')), parts along dimension 0, may hold values from -6 to 6
- value_tan: bfloat16 [16384, 24, 128], P(('clip', 'ctx', 'head')), parts along dimension 0, may hold values from -6 to 6
- used_tiles: int32 [32, 16, 2], P(('clip', 'ctx')), parts along dimension 0, may hold values from 0 to 3, as said below
- picked_slots: int32 [128, 8], P(('clip', 'ctx')), parts along dimension 0, may hold values from 0 to 31, as said below
- tile_count: int32 [128], P(('clip', 'ctx')), parts along dimension 0, may hold values from 4 to 8
Outputs:
- attended: bfloat16 [16384, 24, 128], P(('clip', 'ctx', 'head')), parts along dimension 0
- attended_tan: bfloat16 [16384, 24, 128], P(('clip', 'ctx', 'head')), parts along dimension 0
The draws below stay inside these ranges and needn't reach their ends.
There are 2 independent parts, one for each index of `clip`. The reference program is written for one: setup_inputs(seed, part) draws one part's arguments, and reference() takes and returns one part's arrays. A program takes and returns all parts, laid end to end along the dimension named above; each array names one. Nothing has to cross between parts.
Inputs may be any that keep to these rules, and one draw needn't show every extreme that they name: `used_tiles`: for each a and c the 2 entries are different tile numbers. `picked_slots`: each row holds 8 different entries.
All inputs are finite; a program needn't handle non-finite values.
Results may differ from the reference program's by a relative error of at most 0.011.
Values may be sent and summed in bfloat16 or wider, within the bound.
No kernel may reach another device: no remote copies, remote signals or barrier semaphores. Data moves between devices by JAX's collectives and lax.ppermute only.
A program may use at most 128 MiB of HBM per device.

```python
import jax
import jax.numpy as jnp
from jax import lax

H = 24
DH = 128
TILE = 128
TPS = 4
CAP = 2
SEL = 8
QTILES = 64
S = 8192
N_CTX = 16


def draw_queries(key, part):
    key = jax.random.fold_in(key, 3)
    drawn = jax.random.normal(key, (S, H, DH), jnp.float32)
    return drawn.astype(jnp.bfloat16)


def draw_key_rows(key, part):
    key = jax.random.fold_in(key, 5)
    drawn = jax.random.normal(key, (S, H, DH), jnp.float32)
    return drawn.astype(jnp.bfloat16)


def draw_used_tiles(key, part):
    key = jax.random.fold_in(key, 11)
    subkeys = jax.random.split(key, N_CTX * N_CTX)
    chosen = jax.vmap(lambda sub: jax.random.permutation(sub, TPS)[:CAP])(subkeys)
    return chosen.reshape(N_CTX, N_CTX, CAP).astype(jnp.int32)


def draw_picked_slots(key, part):
    key = jax.random.fold_in(key, 13)
    subkeys = jax.random.split(key, QTILES)
    chosen = jax.vmap(lambda sub: jax.random.permutation(sub, N_CTX * CAP)[:SEL])(subkeys)
    return chosen.astype(jnp.int32)


def draw_tile_count(key, part):
    key = jax.random.fold_in(key, 17)
    counts = jax.random.randint(key, (QTILES,), SEL // 2, SEL + 1)
    return counts.at[0].set(SEL).astype(jnp.int32)


def shard_levels(rng, shape, pieces, low, largest):
    factor_of = 1.0
    for position, blocks in pieces:
        draws = jax.random.uniform(jax.random.fold_in(jax.random.fold_in(rng, 6), position), (blocks,), jnp.float32, low / len(pieces), largest / len(pieces))
        factor_of = factor_of * jnp.repeat(jnp.exp(draws), shape[position] // blocks).reshape((-1,) + (1,) * (len(shape) - 1 - position))
    return factor_of


def bell_draw(rng, dims, spread, limit, cuts=(), kind=jnp.bfloat16):
    entries = jax.random.normal(rng, dims, jnp.float32) * spread
    if len(cuts) > 0:
        entries = shard_levels(rng, dims, cuts, -0.22, 0.18) * entries
    return jnp.clip(entries, min=-limit, max=limit).astype(kind)


def setup_inputs(seed: int = 0, part: int = 0) -> dict:
    seeds = jax.random.split(jax.random.key(seed), 10)
    own_keys = jax.random.split(jax.random.fold_in(seeds[9], part), 10)
    queries = draw_queries(jax.random.fold_in(jax.random.fold_in(seeds[9], part), 71), part)
    key_rows = draw_key_rows(jax.random.fold_in(jax.random.fold_in(seeds[9], part), 71), part)
    values = bell_draw(own_keys[2], (S, H, DH), 1.0, 6.0, ((0, 128),))
    query_tan = bell_draw(own_keys[3], (S, H, DH), 1.0, 6.0, ((0, 128),))
    key_tan = bell_draw(own_keys[4], (S, H, DH), 1.0, 6.0, ((0, 128),))
    value_tan = bell_draw(own_keys[5], (S, H, DH), 1.0, 6.0, ((0, 128),))
    used_tiles = draw_used_tiles(jax.random.fold_in(jax.random.fold_in(seeds[9], part), 71), part)
    picked_slots = draw_picked_slots(jax.random.fold_in(jax.random.fold_in(seeds[9], part), 71), part)
    tile_count = draw_tile_count(jax.random.fold_in(jax.random.fold_in(seeds[9], part), 71), part)
    return dict(queries=queries, key_rows=key_rows, values=values, query_tan=query_tan, key_tan=key_tan, value_tan=value_tan, used_tiles=used_tiles, picked_slots=picked_slots, tile_count=tile_count)


def attend_tiles(query_blk, key_blk, value_blk, query_dir, key_dir, value_dir, live_keys):
    query_f = query_blk.astype(jnp.float32)
    key_f = key_blk.astype(jnp.float32)
    query_df = query_dir.astype(jnp.float32)
    key_df = key_dir.astype(jnp.float32)
    factor = query_blk.shape[-1] ** -0.5
    score = jnp.einsum("bqhd,bkhd->bhqk", query_f, key_f) * factor
    score_dir = (jnp.einsum("bqhd,bkhd->bhqk", query_df, key_f) + jnp.einsum("bqhd,bkhd->bhqk", query_f, key_df)) * factor
    allowed = live_keys[:, None, None, :]
    masked = jnp.where(allowed, score, -jnp.inf)
    row_max = jnp.max(masked, axis=-1, keepdims=True)
    expo = jnp.where(allowed, jnp.exp(masked - row_max), 0.0)
    prob = expo / jnp.sum(expo, axis=-1, keepdims=True)
    centre = jnp.sum(prob * score_dir, axis=-1, keepdims=True)
    prob_dir = prob * (score_dir - centre)
    prob_b = prob.astype(jnp.bfloat16).astype(jnp.float32)
    prob_db = prob_dir.astype(jnp.bfloat16).astype(jnp.float32)
    value_f = value_blk.astype(jnp.float32)
    value_df = value_dir.astype(jnp.float32)
    output = jnp.einsum("bhqk,bkhd->bqhd", prob_b, value_f)
    output_dir = jnp.einsum("bhqk,bkhd->bqhd", prob_db, value_f) + jnp.einsum("bhqk,bkhd->bqhd", prob_b, value_df)
    return output.astype(jnp.bfloat16), output_dir.astype(jnp.bfloat16)


def reference(queries, key_rows, values, query_tan, key_tan, value_tan, used_tiles, picked_slots, tile_count):
    heads = queries.shape[1]
    width = queries.shape[2]
    n_tiles = queries.shape[0] // TILE
    shard_of = (picked_slots // CAP).astype(jnp.int32)
    within = (picked_slots % CAP).astype(jnp.int32)
    owner = (jnp.arange(n_tiles, dtype=jnp.int32) // TPS)[:, None]
    chosen = (shard_of * TPS + used_tiles[owner, shard_of, within]).astype(jnp.int32)
    live_all = (jnp.arange(SEL * TILE, dtype=jnp.int32) // TILE)[None, :] < tile_count[:, None]

    def tiled(array):
        return array.reshape(n_tiles, TILE, heads, width)

    def one_tile(tile_index):
        pick_row = chosen[tile_index]

        def fetch(array):
            return tiled(array)[pick_row].reshape(1, SEL * TILE, heads, width)

        def own(array):
            return lax.dynamic_slice_in_dim(tiled(array), tile_index, 1, 0)

        return attend_tiles(own(queries), fetch(key_rows), fetch(values), own(query_tan),
                            fetch(key_tan), fetch(value_tan), live_all[tile_index][None, :])

    output, output_dir = lax.map(one_tile, jnp.arange(n_tiles, dtype=jnp.int32))
    return output.reshape(queries.shape), output_dir.reshape(queries.shape)
```

```python
import functools

import jax
import jax.numpy as jnp
from jax import lax
from jax.experimental import pallas as pl
from jax.experimental.pallas import tpu as pltpu
from jax.sharding import Mesh, PartitionSpec as P

TILE = 128
ROW = 4
GROUP = 4
LOWEST = -3.0e38
LOG2E = 1.4426950408889634
STAT_ROWS = 16


def shift(count, step):
    return [(i, (i + step) % count) for i in range(count)]


def tile_of(block):
    return block.reshape(block.shape[0] * block.shape[1], block.shape[2])


def dot_nt(left, right):
    return lax.dot_general(
        left, right, (((1,), (1,)), ((), ())), preferred_element_type=jnp.float32
    )


def dot_nn(left, right):
    return jnp.dot(left, right, preferred_element_type=jnp.float32)


def one_pair(query, query_dir, key, key_dir, value, value_dir):
    factor = query.shape[-1] ** (-0.5)
    score = dot_nt(query, key) * (factor * LOG2E)
    score_dir = (
        dot_nt(
            jnp.concatenate([query_dir, query], axis=1), jnp.concatenate([key, key_dir], axis=1)
        )
        * factor
    )
    top = jnp.max(score, axis=1, keepdims=True)
    expo = jnp.exp2(score - top)
    total = jnp.sum(expo, axis=1, keepdims=True)
    centre = jnp.sum(expo * score_dir, axis=1, keepdims=True) / total
    expo_b = expo.astype(jnp.bfloat16)
    expo_db = (expo * (score_dir - centre)).astype(jnp.bfloat16)
    out = dot_nn(expo_b, value)
    out_dir = dot_nn(
        jnp.concatenate([expo_db, expo_b], axis=1), jnp.concatenate([value, value_dir], axis=0)
    )
    return top, total, centre, out, out_dir


def three_parts(number):
    first = number.astype(jnp.bfloat16).astype(jnp.float32)
    rest = number - first
    second = rest.astype(jnp.bfloat16).astype(jnp.float32)
    return first, second, rest - second


def attend_kernel(pairs, *refs):
    key_in, query_in, out_refs = refs[:ROW], refs[ROW : 2 * ROW], refs[2 * ROW : 3 * ROW]
    keys, queries, acc, acc_dir, tops, totals, centres, sem_k, sem_q = refs[3 * ROW :]
    copies = []
    for r in range(ROW):
        copies.append(pltpu.make_async_copy(key_in[r], keys.at[r], sem_k.at[r]))
        copies.append(pltpu.make_async_copy(query_in[r], queries.at[r], sem_q.at[r]))
    for copy in copies:
        copy.start()
    acc[...] = jnp.zeros_like(acc)
    acc_dir[...] = jnp.zeros_like(acc_dir)
    tops[...] = jnp.full_like(tops, LOWEST)
    totals[...] = jnp.zeros_like(totals)
    centres[...] = jnp.zeros_like(centres)
    for copy in copies:
        copy.wait()
    count = pairs[pairs.shape[0] - 1]

    def group(step, carry):
        codes = [pairs[step * GROUP + i] for i in range(GROUP)]
        results = []
        for code in codes:
            key_at, query_at = code & 15, (code >> 4) & 15
            key_block, key_rows = key_at >> 2, pl.ds((key_at & 3) * 2, 2)
            query_block, query_rows = query_at >> 2, pl.ds((query_at & 3) * 2, 2)
            results.append(
                one_pair(
                    tile_of(queries[query_block, query_rows, 0]),
                    tile_of(queries[query_block, query_rows, 1]),
                    tile_of(keys[key_block, key_rows, 0]),
                    tile_of(keys[key_block, key_rows, 1]),
                    tile_of(keys[key_block, key_rows, 2]),
                    tile_of(keys[key_block, key_rows, 3]),
                )
            )
        for code, (top, total, centre, out, out_dir) in zip(codes, results):
            at = code >> 8
            top_0, total_0, centre_0 = tops[at], totals[at], centres[at]
            out_0, out_dir_0 = acc[at], acc_dir[at]
            top_n = jnp.maximum(top, top_0)
            weight_0 = jnp.exp2(top_0 - top_n)
            weight = jnp.exp2(top - top_n)
            part_0, part = weight_0 * total_0, weight * total
            total_n = part_0 + part
            centre_n = (part_0 * centre_0 + part * centre) / total_n
            tops[at], totals[at], centres[at] = top_n, total_n, centre_n
            acc[at] = weight_0 * out_0 + weight * out
            acc_dir[at] = (
                weight_0 * out_dir_0
                + weight * out_dir
                + (weight_0 * (centre_0 - centre_n)) * out_0
                + (weight * (centre - centre_n)) * out
            )
        return carry

    lax.fori_loop(0, (count + GROUP - 1) // GROUP, group, 0)

    lane = lax.broadcasted_iota(jnp.int32, (TILE, TILE), 1)
    for r in range(ROW):

        def finish(t, carry, r=r):
            at = r * ROW + t
            total = totals[at]
            some = total > 0
            inverse = jnp.where(some, 1.0 / jnp.where(some, total, 1.0), 0.0)
            level = jnp.where(some, tops[at] + jnp.log2(jnp.where(some, total, 1.0)), LOWEST)
            out_refs[r][t, 0:TILE] = (acc[at] * inverse).astype(jnp.bfloat16)
            out_refs[r][t, TILE : 2 * TILE] = (acc_dir[at] * inverse).astype(jnp.bfloat16)
            table = jnp.zeros((TILE, TILE), jnp.float32)
            for column, part in enumerate(three_parts(level) + three_parts(centres[at])):
                table = jnp.where(lane == column, part, table)
            table = jnp.transpose(table, (1, 0))
            out_refs[r][t, 2 * TILE :] = table[:STAT_ROWS].astype(jnp.bfloat16)
            return carry

        lax.fori_loop(0, ROW, finish, 0)


def attend(pairs, key_blocks, query_blocks):
    width = key_blocks[0].shape[-1]
    tiles = key_blocks[0].shape[0] // 2
    rows = 2 * TILE + STAT_ROWS
    slots = ROW * tiles + 1
    anywhere = pl.BlockSpec(memory_space=pl.ANY)
    return pl.pallas_call(
        attend_kernel,
        out_shape=[jax.ShapeDtypeStruct((tiles, rows, width), jnp.bfloat16)] * ROW,
        in_specs=[pl.BlockSpec(memory_space=pltpu.SMEM)] + [anywhere] * (2 * ROW),
        out_specs=[pl.BlockSpec(memory_space=pltpu.VMEM)] * ROW,
        scratch_shapes=[
            pltpu.VMEM((ROW,) + key_blocks[0].shape, jnp.bfloat16),
            pltpu.VMEM((ROW,) + query_blocks[0].shape, jnp.bfloat16),
            pltpu.VMEM((slots, TILE, width), jnp.float32),
            pltpu.VMEM((slots, TILE, width), jnp.float32),
            pltpu.VMEM((slots, TILE, 1), jnp.float32),
            pltpu.VMEM((slots, TILE, 1), jnp.float32),
            pltpu.VMEM((slots, TILE, 1), jnp.float32),
            pltpu.SemaphoreType.DMA((ROW,)),
            pltpu.SemaphoreType.DMA((ROW,)),
        ],
        compiler_params=pltpu.CompilerParams(vmem_limit_bytes=32 * 1024 * 1024),
        cost_estimate=pl.CostEstimate(
            flops=5_000_000_000, bytes_accessed=5_000_000, transcendentals=500_000
        ),
        name="attend",
    )(pairs, *key_blocks, *query_blocks)


def combine_kernel(*refs):
    parts, out_ref = refs[:ROW], refs[ROW]
    tiles = parts[0].shape[0]

    def one_tile(t, carry):
        levels, centres = [], []
        for part in parts:
            table = part[t, 2 * TILE :].astype(jnp.float32)
            table = jnp.transpose(
                jnp.concatenate(
                    [table, jnp.zeros((TILE - STAT_ROWS, TILE), jnp.float32)], axis=0
                ),
                (1, 0),
            )
            levels.append(table[:, 0:1] + table[:, 1:2] + table[:, 2:3])
            centres.append(table[:, 3:4] + table[:, 4:5] + table[:, 5:6])
        top = functools.reduce(jnp.maximum, levels)
        weights = [jnp.exp2(level - top) for level in levels]
        inverse = 1.0 / sum(weights)
        weights = [weight * inverse for weight in weights]
        centre = sum(weight * each for weight, each in zip(weights, centres))
        out = jnp.zeros((TILE, parts[0].shape[2]), jnp.float32)
        out_dir = jnp.zeros_like(out)
        for part, weight, each in zip(parts, weights, centres):
            value = part[t, 0:TILE].astype(jnp.float32)
            value_dir = part[t, TILE : 2 * TILE].astype(jnp.float32)
            out = out + weight * value
            out_dir = out_dir + weight * value_dir + (weight * (each - centre)) * value
        half = TILE // 2
        out_ref[pl.ds(2 * t, 2), 0] = out.reshape(2, half, -1).astype(jnp.bfloat16)
        out_ref[pl.ds(2 * t, 2), 1] = out_dir.reshape(2, half, -1).astype(jnp.bfloat16)
        return carry

    lax.fori_loop(0, tiles, one_tile, 0)


def combine(parts):
    tiles, _, width = parts[0].shape
    return pl.pallas_call(
        combine_kernel,
        out_shape=jax.ShapeDtypeStruct((2 * tiles, 2, TILE // 2, width), jnp.bfloat16),
        in_specs=[pl.BlockSpec(memory_space=pltpu.VMEM)] * ROW,
        out_specs=pl.BlockSpec(memory_space=pltpu.VMEM),
        compiler_params=pltpu.CompilerParams(vmem_limit_bytes=16 * 1024 * 1024),
        cost_estimate=pl.CostEstimate(
            flops=1_000_000, bytes_accessed=1_500_000, transcendentals=1000
        ),
        name="combine",
    )(*parts)


def list_pairs(used_tiles, picked_slots, tile_count):
    row, column = lax.axis_index("cy"), lax.axis_index("cx")
    tiles, slots = picked_slots.shape
    capacity = used_tiles.shape[2]
    flat = used_tiles.reshape(-1)
    chosen = picked_slots[..., None] == jnp.arange(flat.shape[0], dtype=jnp.int32)
    tile = jnp.sum(jnp.where(chosen, flat, 0), axis=-1)
    live = jnp.arange(slots, dtype=jnp.int32)[None, :] < tile_count[:, None]
    code = jnp.where(live, picked_slots // capacity * tiles + tile, -1)
    codes = jnp.concatenate(
        [code] + [lax.ppermute(code, "cx", shift(ROW, r)) for r in range(1, ROW)], axis=0
    ).reshape(-1)
    shard = codes // tiles
    valid = (codes >= 0) & (shard % ROW == column)
    key_at = (row - shard // ROW) % ROW * tiles + codes % tiles
    size = codes.shape[0]
    query_at = jnp.arange(size, dtype=jnp.int32) // slots
    entry = (query_at * 16 + query_at) * 16 + key_at
    place = jnp.arange(size, dtype=jnp.int32)
    before = jnp.sum((place[None, :] < place[:, None]) & valid[None, :], axis=1, dtype=jnp.int32)
    wanted = jnp.arange(size + GROUP, dtype=jnp.int32)
    hit = valid[None, :] & (before[None, :] == wanted[:, None])
    count = jnp.sum(valid, dtype=jnp.int32)
    listed = jnp.where(
        wanted < count, jnp.sum(jnp.where(hit, entry[None, :], 0), axis=1), ROW * tiles * 256
    )
    return jnp.concatenate([listed, count[None]])


def body(
    queries, key_rows, values, query_tan, key_tan, value_tan, used_tiles, picked_slots, tile_count
):
    groups = lax.axis_size("head")
    tokens, heads, width = queries.shape
    per_group = heads // groups
    pairs = list_pairs(used_tiles, picked_slots, tile_count)
    stacked = jnp.stack([key_rows, key_tan, values, value_tan, queries, query_tan])
    stacked = stacked.reshape(6, tokens, groups, per_group, width).transpose(3, 2, 0, 1, 4)
    finished = []
    for h in range(per_group):
        moved = lax.all_to_all(stacked[h], "head", split_axis=0, concat_axis=0, tiled=True)
        key_part, query_part = moved[:, :4], moved[:, 4:]
        key_blocks = [key_part] + [
            lax.ppermute(key_part, "cy", shift(ROW, r)) for r in range(1, ROW)
        ]
        query_blocks = [query_part] + [
            lax.ppermute(query_part, "cx", shift(ROW, r)) for r in range(1, ROW)
        ]
        parts = attend(pairs, key_blocks, query_blocks)
        parts = [parts[0]] + [
            lax.ppermute(parts[r], "cx", shift(ROW, -r)) for r in range(1, ROW)
        ]
        whole = combine(parts)
        finished.append(
            lax.all_to_all(whole, "head", split_axis=0, concat_axis=0, tiled=True)
        )
    finished = jnp.stack(finished)
    finished = finished.transpose(2, 3, 1, 0, 4).reshape(2, tokens, heads, width)
    return finished[0], finished[1]


def solution(mesh):
    fine = Mesh(
        mesh.devices.reshape(mesh.devices.shape[0], ROW, ROW, mesh.devices.shape[2]),
        ("clip", "cy", "cx", "head"),
    )
    tokens = P(("clip", "cy", "cx", "head"), None, None)
    shards = ("clip", "cy", "cx")
    return jax.shard_map(
        body,
        mesh=fine,
        in_specs=(tokens,) * 6 + (P(shards, None, None), P(shards, None), P(shards)),
        out_specs=(tokens, tokens),
        check_vma=False,
    )
```
